1024 devices in a mesh: row: 16 (over z, core), col: 64 (over y, x).
Axes of the slice: x: 8, y: 8, z: 8, core: 2. Of those that a mesh axis runs over, the one named last changes fastest.
Arguments:
- users: bfloat16 [16, 64, 32, 128], P('row', 'col'), may hold values from -6 to 6
- items: bfloat16 [64, 16, 128, 128], P('col', 'row'), may hold values from -6 to 6
- user_degree: int32 [16, 64, 32], P('row', 'col'), may hold values from 1 to 16
- item_degree: int32 [64, 16, 128], P('col', 'row'), may hold values from 1 to 16
- tile_values: bfloat16 [16, 64, 48, 128, 128], P('row', 'col'), may hold values from -0.25 to 0.25
- tile_rows: int32 [16, 64, 48], P('row', 'col'), may hold values from 0 to 15
- tile_cols: int32 [16, 64, 48], P('row', 'col'), may hold values from 0 to 15
- tile_count: int32 [16, 64], P('row', 'col'), may hold values from 16 to 48, as said below
- bpr_user: int32 [16, 64, 256], P('row', 'col'), may hold values from 0 to 31
- bpr_pos: int32 [16, 64, 256], P('row', 'col'), may hold values from 0 to 127
- bpr_neg: int32 [16, 64, 256], P('row', 'col'), may hold values from 0 to 127
Outputs:
- user_out: bfloat16 [16, 64, 32, 128], P('row', 'col')
- item_out: bfloat16 [64, 16, 128, 128], P('col', 'row')
- grad_users: float32 [16, 64, 32, 128], P('row', 'col')
- grad_items: float32 [64, 16, 128, 128], P('col', 'row')
The draws below stay inside these ranges and needn't reach their ends.
Inputs may be any that keep to these rules, and one draw needn't show every extreme that they name: `tile_count`: at least a third of the slots are live on every device, and some device has all 48 slots live.
All inputs are finite; a program needn't handle non-finite values.
Results may differ from the reference program's by a relative error of at most 0.0069.
Values may be sent and summed in bfloat16 or wider, within the bound.
A program may use at most 32 MiB of HBM per device.

```python
import jax
import jax.numpy as jnp
from jax import lax

D = 128
TB = 128
UC = 32
IC = 128
TILES = 48
BPR = 256
TROWS = 16
TCOLS = 16
N_ROW = 16
N_COL = 64


def draw_tile_count(key, part):
    key = jax.random.fold_in(key, 11)
    first, second = jax.random.split(key)
    total = N_ROW * N_COL
    counts = jax.random.randint(first, (total,), TILES // 3, TILES + 1)
    chosen = jax.random.randint(second, (), 0, total)
    counts = jnp.where(jnp.arange(total) == chosen, TILES, counts)
    return counts.reshape(N_ROW, N_COL).astype(jnp.int32)


def with_ends(entries, own_key, low, top_value):
    shape = entries.shape
    spot = [jax.random.randint(jax.random.fold_in(own_key, axis), (), 0, shape[axis]) for axis in range(len(shape))]
    entries = entries.at[tuple(spot)].set(low)
    longest = shape.index(max(shape))
    spot[longest] = (spot[longest] + 1) % shape[longest]
    return entries.at[tuple(spot)].set(top_value)


def levels(rng, shape, cuts, low, top_value):
    def one(axis_at, blocks):
        steps = jax.random.uniform(jax.random.fold_in(jax.random.fold_in(rng, 6), axis_at), (blocks,), jnp.float32, low / len(cuts), top_value / len(cuts))
        return jnp.repeat(jnp.exp(steps), shape[axis_at] // blocks).reshape((-1,) + (1,) * (len(shape) - axis_at - 1))

    factor_of = one(*cuts[0])
    for cut in cuts[1:]:
        factor_of = factor_of * one(*cut)
    return factor_of


def gaussian(rng, shape, spread, reach, shards=(), held_as=jnp.bfloat16):
    array = spread * jax.random.normal(rng, shape, jnp.float32)
    if shards:
        array = array * levels(rng, shape, shards, -0.22, 0.18)
    return jnp.clip(array, -reach, reach).astype(held_as)


def setup_inputs(seed: int = 0) -> dict:
    splits = jax.random.split(jax.random.key(seed), 12)
    users = gaussian(splits[0], (N_ROW, N_COL, UC, D), 1.0, 6.0, ((0, 16), (1, 64)))
    items = gaussian(splits[1], (N_COL, N_ROW, IC, D), 1.0, 6.0, ((0, 64), (1, 16)))
    user_degree = with_ends(jax.random.randint(splits[2], (N_ROW, N_COL, UC), 1, 17), jax.random.fold_in(splits[2], 1), 1, 16).astype(jnp.int32)
    item_degree = with_ends(jax.random.randint(splits[3], (N_COL, N_ROW, IC), 1, 17), jax.random.fold_in(splits[3], 1), 1, 16).astype(jnp.int32)
    tile_values = gaussian(splits[4], (N_ROW, N_COL, TILES, TB, TB), (3.0 / (TILES * TB * N_COL // TROWS) ** 0.5), 0.25, ((0, 16), (1, 64)))
    tile_rows = with_ends(jax.random.randint(splits[5], (N_ROW, N_COL, TILES), 0, TROWS), jax.random.fold_in(splits[5], 1), 0, TROWS - 1).astype(jnp.int32)
    tile_cols = with_ends(jax.random.randint(splits[6], (N_ROW, N_COL, TILES), 0, TCOLS), jax.random.fold_in(splits[6], 1), 0, TCOLS - 1).astype(jnp.int32)
    tile_count = draw_tile_count(jax.random.fold_in(splits[11], 71), 0)
    bpr_user = with_ends(jax.random.randint(splits[8], (N_ROW, N_COL, BPR), 0, UC), jax.random.fold_in(splits[8], 1), 0, UC - 1).astype(jnp.int32)
    bpr_pos = with_ends(jax.random.randint(splits[9], (N_ROW, N_COL, BPR), 0, IC), jax.random.fold_in(splits[9], 1), 0, IC - 1).astype(jnp.int32)
    bpr_neg = with_ends(jax.random.randint(splits[10], (N_ROW, N_COL, BPR), 0, IC), jax.random.fold_in(splits[10], 1), 0, IC - 1).astype(jnp.int32)
    return dict(users=users, items=items, user_degree=user_degree, item_degree=item_degree, tile_values=tile_values, tile_rows=tile_rows, tile_cols=tile_cols, tile_count=tile_count, bpr_user=bpr_user, bpr_pos=bpr_pos, bpr_neg=bpr_neg)


def propagate(user_in, item_in, user_scale, item_scale, tile_values, tile_rows, tile_cols, tile_count):
    scaled_users = (user_in.astype(jnp.float32) * user_scale).astype(jnp.bfloat16)
    scaled_items = (item_in.astype(jnp.float32) * item_scale).astype(jnp.bfloat16)
    user_region = scaled_users.reshape(N_ROW, TROWS, TB, D)
    item_region = scaled_items.reshape(N_COL, TCOLS, TB, D)

    def visit(carry, index):
        user_acc, item_acc = carry
        row_id = index // N_COL
        col_id = index % N_COL
        tiles = tile_values[row_id, col_id].astype(jnp.float32)
        rows = tile_rows[row_id, col_id]
        cols = tile_cols[row_id, col_id]
        live = (jnp.arange(TILES) < tile_count[row_id, col_id]).astype(jnp.float32)
        item_blocks = item_region[col_id][cols].astype(jnp.float32)
        user_blocks = user_region[row_id][rows].astype(jnp.float32)
        to_users = jnp.einsum('sab,sbd->sad', tiles, item_blocks, precision=lax.Precision.HIGHEST)
        to_items = jnp.einsum('sab,sad->sbd', tiles, user_blocks, precision=lax.Precision.HIGHEST)
        to_users = to_users * live[:, None, None]
        to_items = to_items * live[:, None, None]
        user_acc = user_acc.at[row_id, rows].add(to_users)
        item_acc = item_acc.at[col_id, cols].add(to_items)
        return ((user_acc, item_acc), None)
    start = (jnp.zeros((N_ROW, TROWS, TB, D), jnp.float32), jnp.zeros((N_COL, TCOLS, TB, D), jnp.float32))
    (user_acc, item_acc), _ = lax.scan(visit, start, jnp.arange(N_ROW * N_COL, dtype=jnp.int32))
    user_res = user_acc.reshape(N_ROW, N_COL, UC, D) * user_scale
    item_res = item_acc.reshape(N_COL, N_ROW, IC, D) * item_scale
    return (user_res, item_res)

def triple_grads(user_local, item_local, who, positive, negative):
    hot_user = (who[:, None] == jnp.arange(user_local.shape[0])[None, :]).astype(jnp.float32)
    hot_pos = (positive[:, None] == jnp.arange(item_local.shape[0])[None, :]).astype(jnp.float32)
    hot_neg = (negative[:, None] == jnp.arange(item_local.shape[0])[None, :]).astype(jnp.float32)
    highest = lax.Precision.HIGHEST
    user_vec = jnp.dot(hot_user, user_local, precision=highest)
    pos_vec = jnp.dot(hot_pos, item_local, precision=highest)
    neg_vec = jnp.dot(hot_neg, item_local, precision=highest)
    score = lax.optimization_barrier(jnp.sum(user_vec * (pos_vec - neg_vec), axis=1))
    weight = jax.nn.sigmoid(-score)[:, None]
    grad_u = jnp.dot(hot_user.T, -weight * (pos_vec - neg_vec), precision=highest)
    grad_i = jnp.dot(hot_pos.T, -weight * user_vec, precision=highest) + jnp.dot(hot_neg.T, weight * user_vec, precision=highest)
    return (grad_u, grad_i)

def reference(users, items, user_degree, item_degree, tile_values, tile_rows, tile_cols, tile_count, bpr_user, bpr_pos, bpr_neg):
    user_scale = lax.rsqrt(user_degree.astype(jnp.float32))[..., None]
    item_scale = lax.rsqrt(item_degree.astype(jnp.float32))[..., None]
    user_res, item_res = propagate(users, items, user_scale, item_scale, tile_values, tile_rows, tile_cols, tile_count)
    user_out = user_res.astype(jnp.bfloat16)
    item_out = item_res.astype(jnp.bfloat16)
    user_local = user_out.astype(jnp.float32)
    item_local = jnp.transpose(item_out.astype(jnp.float32), (1, 0, 2, 3))
    grad_u, grad_i = jax.vmap(jax.vmap(triple_grads))(user_local, item_local, bpr_user, bpr_pos, bpr_neg)
    grad_i = jnp.transpose(grad_i, (1, 0, 2, 3))
    grad_users, grad_items = propagate(grad_u, grad_i, user_scale, item_scale, tile_values, tile_rows, tile_cols, tile_count)
    return (user_out, item_out, grad_users, grad_items)
```

```python
import jax
import jax.numpy as jnp
from jax import lax
from jax.experimental import pallas as pl
from jax.experimental.pallas import tpu as pltpu
from jax.sharding import PartitionSpec as P

MESH = pl.DeviceIdType.MESH
F32, BF16, I32 = jnp.float32, jnp.bfloat16, jnp.int32
D = 128
TB = 128
UC = 32
HU = UC // 2
IC = 128
TILES = 48
BPR = 256
NX, NY, NZ = 8, 8, 8
TROWS = NX * NY * UC // TB
TCOLS = NZ * 2 * IC // TB
STOP = 99

SEM = pltpu.SemaphoreType.DMA


def each(n, body):
    lax.fori_loop(0, n, lambda i, c: (body(i), c)[1], 0)


def await_bytes(ref, sem):
    pltpu.make_async_copy(ref, ref, sem).wait()


def column(row, n, start=0):
    i = lax.broadcasted_iota(I32, (n, n), 0)
    j = lax.broadcasted_iota(I32, (n, n), 1)
    return jnp.sum(jnp.where(i == j, jnp.broadcast_to(row, (n, n)), 0), axis=1, keepdims=True)


def inv_sqrt(x):
    y = lax.rsqrt(x)
    return y * (1.5 - 0.5 * x * y * y)


def slot_order(key_row, other_row, live, order_ref):
    n = TILES
    key_row = jnp.where(live, key_row, 1024)
    key = column(key_row, n)
    other = column(other_row, n)
    sub = lax.broadcasted_iota(I32, (n, n), 0)
    lane = lax.broadcasted_iota(I32, (n, n), 1)
    rows = jnp.broadcast_to(key_row, (n, n))
    tied = (rows == key) & (lane < sub)
    rank = jnp.sum(jnp.where((rows < key) | tied, 1, 0), axis=1, keepdims=True)
    follows = jnp.max(jnp.where(tied, 1, 0), axis=1, keepdims=True)
    place = lax.broadcasted_iota(I32, (n, 128), 1)
    slot = lax.broadcasted_iota(I32, (n, 128), 0)
    hit = place == rank
    order_ref[0:1, :] = jnp.sum(jnp.where(hit, slot, 0), axis=0, keepdims=True)
    order_ref[1:2, :] = jnp.sum(jnp.where(hit, other, 0), axis=0, keepdims=True)
    order_ref[2:3, :] = jnp.sum(jnp.where(hit, follows, 0), axis=0, keepdims=True)
    upto = jnp.sum(jnp.where(key <= place, 1, 0), axis=0, keepdims=True)
    order_ref[3:4, :] = jnp.maximum(upto - 1, 0)
    order_ref[4:5, :] = jnp.max(jnp.where(key == place, 1, 0), axis=0, keepdims=True)


def kernel(
    users, items, udeg, ideg, tiles, trows, tcols, tcount, bu, bp, bn,
    user_out, item_out, grad_users, grad_items,
    tv, tt, ordr_v, ordc_v, ordr, ordc, part,
    huT, hu, hdT, hd, upad,
    uf0, uf1, itf0, itf1,
    pu0, pu1, pi0, pi1,
    ra0, rb0, ra1, rb1,
    sa0, sb0, sa1, sb1,
    qa0, qb0, qa1, qb1,
    rp0, rp1, si0, si1, si1f, rz0, rz1,
    load_sem, ag_sem, ag_zs, rs_sem, rs_ps,
):
    r = lax.axis_index("row")
    c = lax.axis_index("col")
    core = lax.rem(r, 2)
    z = lax.div(r, 2)
    x = lax.rem(c, NX)
    y = lax.div(c, NX)

    def at_x(k):
        xx = lax.rem(x + k, NX)
        return xx, (r, y * NX + xx)

    def at_y(k):
        yy = lax.rem(y + k, NY)
        return yy, (r, yy * NX + x)

    def at_z(k):
        zz = lax.rem(z + k, NZ)
        return zz, (zz * 2 + core, c)

    partner = (z * 2 + 1 - core, c)

    def send(src, dst, ssem, rsem, device):
        pltpu.make_async_remote_copy(
            src_ref=src, dst_ref=dst, send_sem=ssem, recv_sem=rsem, device_id=device, device_id_type=MESH
        ).start()

    tile_load = pltpu.make_async_copy(tiles, tv, load_sem)
    tile_load.start()

    barrier = pltpu.get_barrier_semaphore()

    def greet(device):
        pl.semaphore_signal(barrier, inc=1, device_id=device, device_id_type=MESH)

    greet(partner)
    each(NX - 1, lambda k: greet(at_x(k + 1)[1]))
    each(NY - 1, lambda k: greet(at_y(k + 1)[1]))
    each(NZ - 1, lambda k: greet(at_z(k + 1)[1]))

    du = inv_sqrt(column(udeg[...], UC).astype(F32))
    di = inv_sqrt(column(ideg[...], IC).astype(F32))

    def gather_start(q, uf, itf, user_val, item_val):
        uf[y, x] = (user_val * du).astype(BF16)
        itf[z, core] = (item_val * di).astype(BF16)
        if q == 0:
            pl.semaphore_wait(barrier, NX + NY + NZ - 2)
        s = ag_sem.at[q]

        def one_z(k):
            zz, dev = at_z(k + 1)
            own = itf.at[z, core]
            send(own, own, s.at[0], ag_zs.at[q, k], dev)

        def one_x(k):
            own = uf.at[y, x, 0:HU]
            send(own, own, s.at[3], s.at[4], at_x(k + 1)[1])

        def one_y(k):
            own = uf.at[y, x, HU:UC]
            send(own, own, s.at[5], s.at[6], at_y(k + 1)[1])

        each(NX - 1, one_x)
        each(NY - 1, one_y)
        each(NZ - 1, one_z)
        own = itf.at[z, core]
        send(own, own, s.at[1], s.at[2], partner)

    def gather_second(q, uf):
        s = ag_sem.at[q]
        await_bytes(uf.at[0, 0 : NX - 1, 0:HU], s.at[4])

        def one_y(k):
            own = uf.at[y, :, 0:HU]
            send(own, own, s.at[7], s.at[8], at_y(k + 1)[1])

        each(NY - 1, one_y)
        await_bytes(uf.at[0 : NY - 1, 0, HU:UC], s.at[6])

        def one_x(k):
            own = uf.at[:, x, HU:UC]
            send(own, own, s.at[9], s.at[10], at_x(k + 1)[1])

        each(NX - 1, one_x)

    def gather_forward(q, itf):
        s = ag_sem.at[q]

        def one(k):
            zz = lax.rem(z + NZ - 1 - k, NZ)
            got = itf.at[zz, core]
            await_bytes(got, ag_zs.at[q, k])
            send(got, got, s.at[1], s.at[2], partner)

        each(NZ - 1, one)

    def gather_items_done(q, itf):
        await_bytes(itf.at[:, 0], ag_sem.at[q, 2])

    def gather_users_done(q, uf):
        await_bytes(uf.at[0 : NY - 1, :, 0:HU], ag_sem.at[q, 8])
        await_bytes(uf.at[:, 0 : NX - 1, HU:UC], ag_sem.at[q, 10])

    def gather_sent(q, uf, itf):
        s = ag_sem.at[q]
        await_bytes(itf.at[0 : NZ - 1, 0], s.at[0])
        await_bytes(itf.at[:, 0], s.at[1])
        await_bytes(uf.at[0, 0 : NX - 1, 0:HU], s.at[3])
        await_bytes(uf.at[0 : NY - 1, 0, HU:UC], s.at[5])
        await_bytes(uf.at[0 : NY - 1, :, 0:HU], s.at[7])
        await_bytes(uf.at[:, 0 : NX - 1, HU:UC], s.at[9])

    def user_side(itf, pu):
        def one(j, acc):
            other = ordr[1, j]
            block = itf[lax.div(other, 2), lax.rem(other, 2)]
            prod = jnp.dot(tv[ordr[0, j]], block, preferred_element_type=F32)
            acc = acc * ordr[2, j].astype(F32) + prod
            part[j] = acc
            return acc

        lax.fori_loop(0, TILES, one, jnp.zeros((TB, D), F32), unroll=4)

        def place(t):
            whole = part[ordr[3, t]] * ordr[4, t].astype(F32)
            per = NX * UC // TB
            cols = TB // UC
            yy = lax.div(t, per)
            xx = lax.rem(t, per) * cols
            pu[yy, pl.ds(xx, cols)] = whole.reshape(cols, UC, D).astype(pu.dtype)

        each(TROWS, place)

    def item_side(uf, pi):
        def one(j, acc):
            t = ordc[1, j]
            per = NX * UC // TB
            cols = TB // UC
            block = uf[lax.div(t, per), pl.ds(lax.rem(t, per) * cols, cols)].reshape(TB, D)
            prod = jnp.dot(tt[j], block, preferred_element_type=F32)
            acc = acc * ordc[2, j].astype(F32) + prod
            part[j] = acc
            return acc

        lax.fori_loop(0, TILES, one, jnp.zeros((TB, D), F32), unroll=4)

        def place(t):
            pi[lax.div(t, 2), lax.rem(t, 2)] = part[ordc[3, t]] * ordc[4, t].astype(F32)

        each(TCOLS, place)

    def scatter_users_first(q, pu, ra, rb):
        s = rs_sem.at[q]

        def one_y(k):
            yy, dev = at_y(k + 1)
            send(pu.at[yy, :, 0:HU], ra.at[k], s.at[0], s.at[1], dev)

        def one_x(k):
            xx, dev = at_x(k + 1)
            send(pu.at[:, xx, HU:UC], rb.at[k], s.at[2], s.at[3], dev)

        each(NY - 1, one_y)
        each(NX - 1, one_x)

    def scatter_users_second(q, pu, ra, rb, sa, sb, qa, qb):
        s = rs_sem.at[q]
        await_bytes(ra, s.at[1])
        sa[...] = pu[y, :, 0:HU].astype(F32) + jnp.sum(ra[...].astype(F32), axis=0)

        def one_x(k):
            xx, dev = at_x(k + 1)
            send(sa.at[xx], qa.at[k], s.at[4], s.at[5], dev)

        each(NX - 1, one_x)
        await_bytes(rb, s.at[3])
        sb[...] = pu[:, x, HU:UC].astype(F32) + jnp.sum(rb[...].astype(F32), axis=0)

        def one_y(k):
            yy, dev = at_y(k + 1)
            send(sb.at[yy], qb.at[k], s.at[6], s.at[7], dev)

        each(NY - 1, one_y)

    def scatter_users_done(q, sa, sb, qa, qb):
        s = rs_sem.at[q]
        await_bytes(qa, s.at[5])
        await_bytes(qb, s.at[7])
        first = sa[x] + jnp.sum(qa[...], axis=0)
        second = sb[y] + jnp.sum(qb[...], axis=0)
        return jnp.concatenate([first, second], axis=0) * du

    def scatter_users_sent(q, ra, rb, qa, qb):
        s = rs_sem.at[q]
        await_bytes(ra, s.at[0])
        await_bytes(rb, s.at[2])
        await_bytes(qa, s.at[4])
        await_bytes(qb, s.at[6])

    def scatter_items_first(q, pi, rp):
        s = rs_sem.at[q]

        def one(k):
            zz = lax.rem(z + 1 + k, NZ)
            send(pi.at[zz, 1 - core], rp.at[zz], s.at[8], rs_ps.at[q, k], partner)

        each(NZ, one)

    def scatter_items_second(q, pi, rp, si, keep, rz):
        s = rs_sem.at[q]

        def one(k):
            zz, dev = at_z(k + 1)
            await_bytes(rp.at[zz], rs_ps.at[q, k])
            si[zz] = (pi[zz, core] + rp[zz]).astype(si.dtype)
            send(si.at[zz], rz.at[k], s.at[9], s.at[10], dev)

        each(NZ - 1, one)
        await_bytes(rp.at[z], rs_ps.at[q, NZ - 1])
        keep[...] = pi[z, core] + rp[z]

    def scatter_items_done(q, keep, rz):
        await_bytes(rz, rs_sem.at[q, 10])
        return (keep[...] + jnp.sum(rz[...].astype(F32), axis=0)) * di

    def scatter_items_sent(q, rp, rz):
        await_bytes(rp, rs_sem.at[q, 8])
        await_bytes(rz, rs_sem.at[q, 9])

    gather_start(0, uf0, itf0, users[...].astype(F32), items[...].astype(F32))
    live = lax.broadcasted_iota(I32, (1, TILES), 1) < tcount[0, 0]
    slot_order(trows[...], tcols[...], live, ordr_v)
    slot_order(tcols[...], trows[...], live, ordc_v)
    copy_r = pltpu.make_async_copy(ordr_v, ordr, load_sem)
    tile_load.wait()
    copy_r.start()
    copy_r.wait()
    copy_c = pltpu.make_async_copy(ordc_v, ordc, load_sem)
    copy_c.start()
    copy_c.wait()
    gather_second(0, uf0)
    gather_forward(0, itf0)

    def turn(j):
        tt[j] = tv[ordc[0, j]].T

    each(TILES, turn)

    ids = lax.broadcasted_iota(I32, (IC, BPR), 0)
    hot_u = jnp.where(ids == bu[...], 1.0, 0.0)
    hot_d = jnp.where(ids == bp[...], 1.0, 0.0) - jnp.where(ids == bn[...], 1.0, 0.0)
    huT[...] = hot_u[0:UC].astype(BF16)
    hdT[...] = hot_d.astype(BF16)
    hu[...] = hot_u.T.astype(BF16)
    hd[...] = hot_d.T.astype(BF16)

    gather_items_done(0, itf0)
    user_side(itf0, pu0)
    scatter_users_first(0, pu0, ra0, rb0)
    gather_users_done(0, uf0)
    item_side(uf0, pi0)
    scatter_items_first(0, pi0, rp0)
    scatter_users_second(0, pu0, ra0, rb0, sa0, sb0, qa0, qb0)
    scatter_items_second(0, pi0, rp0, si0, si0.at[z], rz0)
    u_out = scatter_users_done(0, sa0, sb0, qa0, qb0).astype(BF16)
    i_out = scatter_items_done(0, si0.at[z], rz0).astype(BF16)
    user_out[...] = u_out
    item_out[...] = i_out

    upad[0:UC] = u_out
    upad[UC:IC] = jnp.zeros((IC - UC, D), BF16)
    u_vec = jnp.dot(hu[...], upad[...], preferred_element_type=F32)
    d_vec = jnp.dot(hd[...], i_out, preferred_element_type=F32)
    score = jnp.sum(u_vec * d_vec, axis=1, keepdims=True)
    weight = -jax.nn.sigmoid(-score)

    def spread(hotT, v):
        hi = v.astype(BF16)
        lo = (v - hi.astype(F32)).astype(BF16)
        return jnp.dot(hotT, hi, preferred_element_type=F32) + jnp.dot(hotT, lo, preferred_element_type=F32)

    g_u = spread(huT[...], weight * d_vec)
    g_i = spread(hdT[...], weight * u_vec)

    gather_start(1, uf1, itf1, g_u, g_i)
    gather_second(1, uf1)
    gather_forward(1, itf1)
    gather_items_done(1, itf1)
    user_side(itf1, pu1)
    scatter_users_first(1, pu1, ra1, rb1)
    gather_users_done(1, uf1)
    item_side(uf1, pi1)
    scatter_items_first(1, pi1, rp1)
    scatter_users_second(1, pu1, ra1, rb1, sa1, sb1, qa1, qb1)
    scatter_items_second(1, pi1, rp1, si1, si1f, rz1)
    grad_users[...] = scatter_users_done(1, sa1, sb1, qa1, qb1)
    grad_items[...] = scatter_items_done(1, si1f, rz1)

    gather_sent(0, uf0, itf0)
    gather_sent(1, uf1, itf1)
    scatter_users_sent(0, ra0, rb0, qa0, qb0)
    scatter_users_sent(1, ra1, rb1, qa1, qb1)
    scatter_items_sent(0, rp0, rz0)
    scatter_items_sent(1, rp1, rz1)


def local(users, items, udeg, ideg, tiles, trows, tcols, tcount, bu, bp, bn):
    vmem = pl.BlockSpec(memory_space=pltpu.VMEM)
    smem = pl.BlockSpec(memory_space=pltpu.SMEM)
    hbm = pl.BlockSpec(memory_space=pl.ANY)
    V = pltpu.VMEM
    order = (8, 128)
    fields = (NY, NX, UC, D)
    fieldi = (NZ, 2, IC, D)
    outs = pl.pallas_call(
        kernel,
        out_shape=(
            jax.ShapeDtypeStruct((UC, D), BF16),
            jax.ShapeDtypeStruct((IC, D), BF16),
            jax.ShapeDtypeStruct((UC, D), F32),
            jax.ShapeDtypeStruct((IC, D), F32),
        ),
        in_specs=[vmem, vmem, vmem, vmem, hbm, vmem, vmem, smem, vmem, vmem, vmem],
        out_specs=(vmem,) * 4,
        scratch_shapes=[
            V((TILES, TB, TB), BF16),
            V((TILES, TB, TB), BF16),
            V(order, I32),
            V(order, I32),
            pltpu.SMEM(order, I32),
            pltpu.SMEM(order, I32),
            V((TILES, TB, D), F32),
            V((UC, BPR), BF16),
            V((BPR, IC), BF16),
            V((IC, BPR), BF16),
            V((BPR, IC), BF16),
            V((IC, D), BF16),
            V(fields, BF16),
            V(fields, BF16),
            V(fieldi, BF16),
            V(fieldi, BF16),
            V(fields, F32),
            V(fields, BF16),
            V(fieldi, F32),
            V(fieldi, F32),
            V((NY - 1, NX, HU, D), F32),
            V((NX - 1, NY, HU, D), F32),
            V((NY - 1, NX, HU, D), BF16),
            V((NX - 1, NY, HU, D), BF16),
            V((NX, HU, D), F32),
            V((NY, HU, D), F32),
            V((NX, HU, D), F32),
            V((NY, HU, D), F32),
            V((NX - 1, HU, D), F32),
            V((NY - 1, HU, D), F32),
            V((NX - 1, HU, D), F32),
            V((NY - 1, HU, D), F32),
            V((NZ, IC, D), F32),
            V((NZ, IC, D), F32),
            V((NZ, IC, D), F32),
            V((NZ, IC, D), BF16),
            V((IC, D), F32),
            V((NZ - 1, IC, D), F32),
            V((NZ - 1, IC, D), BF16),
            SEM,
            SEM((2, 11)),
            SEM((2, NZ - 1)),
            SEM((2, 11)),
            SEM((2, NZ)),
        ],
        compiler_params=pltpu.CompilerParams(
            collective_id=0, has_side_effects=True, vmem_limit_bytes=48 * 1024 * 1024
        ),
        name="lightgcn",
    )(
        users[0, 0], items[0, 0], udeg[0], ideg[0], tiles[0, 0], trows[0], tcols[0], tcount, bu[0], bp[0], bn[0]
    )
    return tuple(o[None, None] for o in outs)


def solution(mesh):
    u2, i2 = P("row", "col"), P("col", "row")
    return jax.shard_map(
        local,
        mesh=mesh,
        in_specs=(u2, i2, u2, i2, u2, u2, u2, u2, u2, u2, u2),
        out_specs=(u2, i2, u2, i2),
        check_vma=False,
    )
```

```python
import jax
import jax.numpy as jnp
from jax import lax
from jax.experimental import pallas as pl
from jax.experimental.pallas import tpu as pltpu
from jax.sharding import PartitionSpec as P

MESH = pl.DeviceIdType.MESH
F32, BF16, I32 = jnp.float32, jnp.bfloat16, jnp.int32
D = 128
TB = 128
UC = 32
HU = UC // 2
IC = 128
TILES = 48
BPR = 256
NX, NY, NZ = 8, 8, 8
TROWS = NX * NY * UC // TB
TCOLS = NZ * 2 * IC // TB

NEAR_FIRST = (0, 6, 1, 5, 2, 4, 3)
FAR_FIRST = (2, 1, 3, 0)
UNROLL = 16

SEM = pltpu.SemaphoreType.DMA


def each(n, body):
    lax.fori_loop(0, n, lambda i, c: (body(i), c)[1], 0)


def each_far_first(n, body):
    def one(i):
        off = lax.div(i + 1, 2)
        body(n // 2 + off * (1 - 2 * lax.rem(i, 2)))

    each(n, one)


def await_bytes(ref, sem):
    pltpu.make_async_copy(ref, ref, sem).wait()


def column(row, n, start=0):
    i = lax.broadcasted_iota(I32, (n, n), 0)
    j = lax.broadcasted_iota(I32, (n, n), 1)
    return jnp.sum(jnp.where(i == j, jnp.broadcast_to(row, (n, n)), 0), axis=1, keepdims=True)


def inv_sqrt(x):
    y = lax.rsqrt(x)
    return y * (1.5 - 0.5 * x * y * y)


def slot_order(key_row, other_row, live, order_ref):
    n = TILES
    key_row = jnp.where(live, key_row, 1024)
    key = column(key_row, n)
    other = column(other_row, n)
    sub = lax.broadcasted_iota(I32, (n, n), 0)
    lane = lax.broadcasted_iota(I32, (n, n), 1)
    rows = jnp.broadcast_to(key_row, (n, n))
    tied = (rows == key) & (lane < sub)
    rank = jnp.sum(jnp.where((rows < key) | tied, 1, 0), axis=1, keepdims=True)
    follows = jnp.max(jnp.where(tied, 1, 0), axis=1, keepdims=True)
    place = lax.broadcasted_iota(I32, (n, 128), 1)
    slot = lax.broadcasted_iota(I32, (n, 128), 0)
    hit = place == rank
    order_ref[0:1, :] = jnp.sum(jnp.where(hit, slot, 0), axis=0, keepdims=True)
    order_ref[1:2, :] = jnp.sum(jnp.where(hit, other, 0), axis=0, keepdims=True)
    order_ref[2:3, :] = jnp.sum(jnp.where(hit, follows, 0), axis=0, keepdims=True)
    upto = jnp.sum(jnp.where(key <= place, 1, 0), axis=0, keepdims=True)
    order_ref[3:4, :] = jnp.maximum(upto - 1, 0)
    order_ref[4:5, :] = jnp.max(jnp.where(key == place, 1, 0), axis=0, keepdims=True)


def kernel(
    users_h, items_h, udeg_h, ideg_h, tiles_h, trows_h, tcols_h, tcount_h, bu_h, bp_h, bn_h,
    user_out, item_out, grad_users, grad_items,
    users, items, udeg, ideg, tv, trows, tcols, tcount, bu, bp, bn,
    tt, ordr_v, ordc_v, ordr, ordc, part,
    huT, hu, hdT, hd, upad,
    uf0, uf1, itf0, itf1,
    pu0, pu1, pi0, pi1,
    ra0, rb0, ra1, rb1,
    sa0, sb0, sa1, sb1,
    qa0, qb0, qa1, qb1,
    rp0, rp1, si0, si1, si1f, rz0, rz1,
    load_sem, ag_sem, ag_xs, ag_ys, ag_zs, rs_sem, rs_as, rs_bs, rs_ps,
):
    r = lax.axis_index("row")
    c = lax.axis_index("col")
    core = lax.rem(r, 2)
    z = lax.div(r, 2)
    x = lax.rem(c, NX)
    y = lax.div(c, NX)

    def at_x(k):
        xx = lax.rem(x + k, NX)
        return xx, (r, y * NX + xx)

    def at_y(k):
        yy = lax.rem(y + k, NY)
        return yy, (r, yy * NX + x)

    def at_z(k):
        zz = lax.rem(z + k, NZ)
        return zz, (zz * 2 + core, c)

    partner = (z * 2 + 1 - core, c)

    def send(src, dst, ssem, rsem, device):
        pltpu.make_async_remote_copy(
            src_ref=src, dst_ref=dst, send_sem=ssem, recv_sem=rsem, device_id=device, device_id_type=MESH
        ).start()

    pairs = (
        (users_h, users), (items_h, items), (udeg_h, udeg), (ideg_h, ideg), (tiles_h, tv), (trows_h, trows),
        (tcols_h, tcols), (tcount_h, tcount), (bu_h, bu), (bp_h, bp), (bn_h, bn),
    )
    loads = [pltpu.make_async_copy(src, dst, load_sem.at[n]) for n, (src, dst) in enumerate(pairs)]
    for n in (2, 3, 0, 1, 5, 6, 7, 4, 8, 9, 10):
        loads[n].start()

    barrier = pltpu.get_barrier_semaphore()

    def greet(device):
        pl.semaphore_signal(barrier, inc=1, device_id=device, device_id_type=MESH)

    greet(partner)
    each(NX - 1, lambda k: greet(at_x(k + 1)[1]))
    each(NY - 1, lambda k: greet(at_y(k + 1)[1]))
    each(NZ - 1, lambda k: greet(at_z(k + 1)[1]))

    for n in range(4):
        loads[n].wait()
    du = inv_sqrt(column(udeg[...], UC).astype(F32))
    di = inv_sqrt(column(ideg[...], IC).astype(F32))

    def gather_start(q, uf, itf, user_val, item_val):
        uf[y, x] = (user_val * du).astype(BF16)
        itf[z, core] = (item_val * di).astype(BF16)
        if q == 0:
            pl.semaphore_wait(barrier, NX + NY + NZ - 2)
        s = ag_sem.at[q]
        mine_u = uf.at[y, x]
        mine_i = itf.at[z, core]

        def one(k):
            send(mine_u, mine_u, s.at[3], ag_xs.at[q, k], at_x(k + 1)[1])
            send(mine_u, mine_u, s.at[5], ag_ys.at[q, k], at_y(k + 1)[1])

        each_far_first(NX - 1, one)
        each_far_first(NZ - 1, lambda k: send(mine_i, mine_i, s.at[0], ag_zs.at[q, k], at_z(k + 1)[1]))
        send(mine_i, mine_i, s.at[1], s.at[2], partner)

    def gather_second(q, uf):
        s = ag_sem.at[q]
        for k in NEAR_FIRST:
            xx = lax.rem(x + NX - 1 - k, NX)
            await_bytes(uf.at[y, xx], ag_xs.at[q, k])
            half = uf.at[y, xx, 0:HU]
            each_far_first(NY - 1, lambda j: send(half, half, s.at[7], s.at[8], at_y(j + 1)[1]))
            yy = lax.rem(y + NY - 1 - k, NY)
            await_bytes(uf.at[yy, x], ag_ys.at[q, k])
            other = uf.at[yy, x, HU:UC]
            each_far_first(NX - 1, lambda j: send(other, other, s.at[9], s.at[10], at_x(j + 1)[1]))

    def gather_forward(q, itf):
        s = ag_sem.at[q]
        for k in NEAR_FIRST:
            zz = lax.rem(z + NZ - 1 - k, NZ)
            got = itf.at[zz, core]
            await_bytes(got, ag_zs.at[q, k])
            send(got, got, s.at[1], s.at[2], partner)

    def gather_items_done(q, itf):
        await_bytes(itf.at[:, 0], ag_sem.at[q, 2])

    def gather_users_done(q, uf):
        await_bytes(uf.at[0 : NY - 1, 0 : NX - 1, 0:HU], ag_sem.at[q, 8])
        await_bytes(uf.at[0 : NY - 1, 0 : NX - 1, HU:UC], ag_sem.at[q, 10])

    def gather_sent(q, uf, itf):
        s = ag_sem.at[q]
        await_bytes(itf.at[0 : NZ - 1, 0], s.at[0])
        await_bytes(itf.at[:, 0], s.at[1])
        await_bytes(uf.at[0, 0 : NX - 1], s.at[3])
        await_bytes(uf.at[0 : NY - 1, 0], s.at[5])
        await_bytes(uf.at[0 : NY - 1, 0 : NX - 1, 0:HU], s.at[7])
        await_bytes(uf.at[0 : NY - 1, 0 : NX - 1, HU:UC], s.at[9])

    def user_side(itf, pu):
        def one(j, acc):
            other = ordr[1, j]
            block = itf[lax.div(other, 2), lax.rem(other, 2)]
            prod = jnp.dot(tv[ordr[0, j]], block, preferred_element_type=F32)
            acc = acc * ordr[2, j].astype(F32) + prod
            part[j] = acc
            return acc

        lax.fori_loop(0, TILES, one, jnp.zeros((TB, D), F32), unroll=UNROLL)

        def place(t):
            whole = part[ordr[3, t]] * ordr[4, t].astype(F32)
            per = NX * UC // TB
            cols = TB // UC
            yy = lax.div(t, per)
            xx = lax.rem(t, per) * cols
            pu[yy, pl.ds(xx, cols)] = whole.reshape(cols, UC, D).astype(pu.dtype)

        each(TROWS, place)

    def item_side(uf, pi):
        def one(j, acc):
            t = ordc[1, j]
            per = NX * UC // TB
            cols = TB // UC
            block = uf[lax.div(t, per), pl.ds(lax.rem(t, per) * cols, cols)].reshape(TB, D)
            prod = jnp.dot(tt[j], block, preferred_element_type=F32)
            acc = acc * ordc[2, j].astype(F32) + prod
            part[j] = acc
            return acc

        lax.fori_loop(0, TILES, one, jnp.zeros((TB, D), F32), unroll=UNROLL)

        def place(t):
            pi[lax.div(t, 2), lax.rem(t, 2)] = part[ordc[3, t]] * ordc[4, t].astype(F32)

        each(TCOLS, place)

    def scatter_users_first(q, pu, ra, rb):
        s = rs_sem.at[q]
        for step in FAR_FIRST:
            px = lax.rem(lax.div(x, 2) + step, NX // 2)
            py = lax.rem(lax.div(y, 2) + step, NY // 2)

            def one(k):
                yy, dev = at_y(k + 1)
                send(pu.at[yy, pl.ds(px * 2, 2), 0:HU], ra.at[px, k], s.at[0], rs_as.at[q, px], dev)
                xx, dev = at_x(k + 1)
                send(pu.at[pl.ds(py * 2, 2), xx, HU:UC], rb.at[py, k], s.at[2], rs_bs.at[q, py], dev)

            each_far_first(NY - 1, one)

    def scatter_users_second(q, pu, ra, rb, sa, sb, qa, qb):
        s = rs_sem.at[q]
        for step in FAR_FIRST:
            px = lax.rem(lax.div(x, 2) + step, NX // 2)
            py = lax.rem(lax.div(y, 2) + step, NY // 2)

            def to_x(xx):
                k = lax.rem(xx - x + NX, NX) - 1
                send(sa.at[xx], qa.at[k], s.at[4], s.at[5], (r, y * NX + xx))

            def to_y(yy):
                k = lax.rem(yy - y + NY, NY) - 1
                send(sb.at[yy], qb.at[k], s.at[6], s.at[7], (r, yy * NX + x))

            await_bytes(ra.at[px], rs_as.at[q, px])
            two = pl.ds(px * 2, 2)
            sa[two] = pu[y, two, 0:HU].astype(F32) + jnp.sum(ra[px].astype(F32), axis=0)
            if step:
                to_x(px * 2)
                to_x(px * 2 + 1)
            else:
                to_x(px * 4 + 1 - x)
            await_bytes(rb.at[py], rs_bs.at[q, py])
            two = pl.ds(py * 2, 2)
            sb[two] = pu[two, x, HU:UC].astype(F32) + jnp.sum(rb[py].astype(F32), axis=0)
            if step:
                to_y(py * 2)
                to_y(py * 2 + 1)
            else:
                to_y(py * 4 + 1 - y)

    def scatter_users_done(q, sa, sb, qa, qb):
        s = rs_sem.at[q]
        await_bytes(qa, s.at[5])
        await_bytes(qb, s.at[7])
        first = sa[x] + jnp.sum(qa[...], axis=0)
        second = sb[y] + jnp.sum(qb[...], axis=0)
        return jnp.concatenate([first, second], axis=0) * du

    def scatter_users_sent(q, ra, rb, qa, qb):
        s = rs_sem.at[q]
        await_bytes(ra, s.at[0])
        await_bytes(rb, s.at[2])
        await_bytes(qa, s.at[4])
        await_bytes(qb, s.at[6])

    def scatter_items_first(q, pi, rp):
        s = rs_sem.at[q]

        def one(k):
            zz = lax.rem(z + 1 + k, NZ)
            send(pi.at[zz, 1 - core], rp.at[zz], s.at[8], rs_ps.at[q, k], partner)

        each_far_first(NZ - 1, one)
        one(NZ - 1)

    def scatter_items_second(q, pi, rp, si, keep, rz):
        s = rs_sem.at[q]

        def one(k):
            zz, dev = at_z(k + 1)
            await_bytes(rp.at[zz], rs_ps.at[q, k])
            si[zz] = (pi[zz, core] + rp[zz]).astype(si.dtype)
            send(si.at[zz], rz.at[k], s.at[9], s.at[10], dev)

        each_far_first(NZ - 1, one)
        await_bytes(rp.at[z], rs_ps.at[q, NZ - 1])
        keep[...] = pi[z, core] + rp[z]

    def scatter_items_done(q, keep, rz):
        await_bytes(rz, rs_sem.at[q, 10])
        return (keep[...] + jnp.sum(rz[...].astype(F32), axis=0)) * di

    def scatter_items_sent(q, rp, rz):
        await_bytes(rp, rs_sem.at[q, 8])
        await_bytes(rz, rs_sem.at[q, 9])

    def products(q, uf, itf, pu, pi, ra, rb, rp, si, keep, rz):
        gather_items_done(q, itf)
        user_side(itf, pu)
        scatter_users_first(q, pu, ra, rb)
        gather_users_done(q, uf)
        item_side(uf, pi)
        scatter_items_first(q, pi, rp)
        scatter_items_second(q, pi, rp, si, keep, rz)

    gather_start(0, uf0, itf0, users[...].astype(F32), items[...].astype(F32))
    for n in range(5, 8):
        loads[n].wait()
    live = lax.broadcasted_iota(I32, (1, TILES), 1) < jnp.broadcast_to(tcount[...], (1, TILES))
    slot_order(trows[...], tcols[...], live, ordr_v)
    slot_order(tcols[...], trows[...], live, ordc_v)
    copy_r = pltpu.make_async_copy(ordr_v, ordr, load_sem.at[11])
    copy_c = pltpu.make_async_copy(ordc_v, ordc, load_sem.at[12])
    copy_r.start()
    copy_c.start()
    gather_second(0, uf0)
    copy_r.wait()
    copy_c.wait()
    loads[4].wait()

    def turn(j):
        tt[j] = tv[ordc[0, j]].T

    each(TILES, turn)
    for n in range(8, 11):
        loads[n].wait()
    ids = lax.broadcasted_iota(I32, (IC, BPR), 0)
    hot_u = jnp.where(ids == bu[...], 1.0, 0.0)
    hot_d = jnp.where(ids == bp[...], 1.0, 0.0) - jnp.where(ids == bn[...], 1.0, 0.0)
    huT[...] = hot_u[0:UC].astype(BF16)
    hdT[...] = hot_d.astype(BF16)
    hu[...] = hot_u.T.astype(BF16)
    hd[...] = hot_d.T.astype(BF16)
    gather_forward(0, itf0)
    products(0, uf0, itf0, pu0, pi0, ra0, rb0, rp0, si0, si0.at[z], rz0)
    scatter_users_second(0, pu0, ra0, rb0, sa0, sb0, qa0, qb0)
    u_out = scatter_users_done(0, sa0, sb0, qa0, qb0).astype(BF16)
    i_out = scatter_items_done(0, si0.at[z], rz0).astype(BF16)
    user_out[...] = u_out
    item_out[...] = i_out

    upad[0:UC] = u_out
    upad[UC:IC] = jnp.zeros((IC - UC, D), BF16)
    u_vec = jnp.dot(hu[...], upad[...], preferred_element_type=F32)
    d_vec = jnp.dot(hd[...], i_out, preferred_element_type=F32)
    score = jnp.sum(u_vec * d_vec, axis=1, keepdims=True)
    weight = -jax.nn.sigmoid(-score)

    def spread(hotT, v):
        hi = v.astype(BF16)
        lo = (v - hi.astype(F32)).astype(BF16)
        return jnp.dot(hotT, hi, preferred_element_type=F32) + jnp.dot(hotT, lo, preferred_element_type=F32)

    g_u = spread(huT[...], weight * d_vec)
    g_i = spread(hdT[...], weight * u_vec)

    gather_start(1, uf1, itf1, g_u, g_i)
    gather_second(1, uf1)
    gather_forward(1, itf1)
    products(1, uf1, itf1, pu1, pi1, ra1, rb1, rp1, si1, si1f, rz1)
    scatter_users_second(1, pu1, ra1, rb1, sa1, sb1, qa1, qb1)
    grad_users[...] = scatter_users_done(1, sa1, sb1, qa1, qb1)
    grad_items[...] = scatter_items_done(1, si1f, rz1)

    gather_sent(0, uf0, itf0)
    gather_sent(1, uf1, itf1)
    scatter_users_sent(0, ra0, rb0, qa0, qb0)
    scatter_users_sent(1, ra1, rb1, qa1, qb1)
    scatter_items_sent(0, rp0, rz0)
    scatter_items_sent(1, rp1, rz1)


def write_out(a, b, c, d, ah, bh, ch, dh, sem):
    copies = [pltpu.make_async_copy(src, dst, sem.at[n]) for n, (src, dst) in enumerate(((a, ah), (b, bh), (c, ch), (d, dh)))]
    for one in copies:
        one.start()
    for one in copies:
        one.wait()


def local(users, items, udeg, ideg, tiles, trows, tcols, tcount, bu, bp, bn):
    vmem = pl.BlockSpec(memory_space=pltpu.VMEM)
    hbm = pl.BlockSpec(memory_space=pltpu.HBM)
    V = pltpu.VMEM
    order = (8, 128)
    fields = (NY, NX, UC, D)
    fieldi = (NZ, 2, IC, D)
    out_shape = (
        jax.ShapeDtypeStruct((UC, D), BF16),
        jax.ShapeDtypeStruct((IC, D), BF16),
        jax.ShapeDtypeStruct((UC, D), F32),
        jax.ShapeDtypeStruct((IC, D), F32),
    )
    args = (users[0, 0], items[0, 0], udeg[0], ideg[0], tiles[0, 0], trows[0], tcols[0], tcount, bu[0], bp[0], bn[0])
    outs = pl.pallas_call(
        kernel,
        out_shape=out_shape,
        in_specs=[hbm] * 11,
        out_specs=(vmem,) * 4,
        scratch_shapes=[V(a.shape, a.dtype) for a in args]
        + [
            V((TILES, TB, TB), BF16),
            V(order, I32),
            V(order, I32),
            pltpu.SMEM(order, I32),
            pltpu.SMEM(order, I32),
            V((TILES, TB, D), F32),
            V((UC, BPR), BF16),
            V((BPR, IC), BF16),
            V((IC, BPR), BF16),
            V((BPR, IC), BF16),
            V((IC, D), BF16),
            V(fields, BF16),
            V(fields, BF16),
            V(fieldi, BF16),
            V(fieldi, BF16),
            V(fields, F32),
            V(fields, BF16),
            V(fieldi, F32),
            V(fieldi, F32),
            V((NX // 2, NY - 1, 2, HU, D), F32),
            V((NY // 2, NX - 1, 2, HU, D), F32),
            V((NX // 2, NY - 1, 2, HU, D), BF16),
            V((NY // 2, NX - 1, 2, HU, D), BF16),
            V((NX, HU, D), F32),
            V((NY, HU, D), F32),
            V((NX, HU, D), F32),
            V((NY, HU, D), F32),
            V((NX - 1, HU, D), F32),
            V((NY - 1, HU, D), F32),
            V((NX - 1, HU, D), F32),
            V((NY - 1, HU, D), F32),
            V((NZ, IC, D), F32),
            V((NZ, IC, D), F32),
            V((NZ, IC, D), F32),
            V((NZ, IC, D), BF16),
            V((IC, D), F32),
            V((NZ - 1, IC, D), F32),
            V((NZ - 1, IC, D), BF16),
            SEM((13,)),
            SEM((2, 11)),
            SEM((2, NX - 1)),
            SEM((2, NY - 1)),
            SEM((2, NZ - 1)),
            SEM((2, 11)),
            SEM((2, NX // 2)),
            SEM((2, NY // 2)),
            SEM((2, NZ)),
        ],
        compiler_params=pltpu.CompilerParams(
            collective_id=0, has_side_effects=True, vmem_limit_bytes=60 * 1024 * 1024
        ),
        name="lightgcn",
    )(*args)
    outs = pl.pallas_call(
        write_out,
        out_shape=out_shape,
        in_specs=[hbm] * 4,
        out_specs=(hbm,) * 4,
        scratch_shapes=[SEM((4,))],
        compiler_params=pltpu.CompilerParams(vmem_limit_bytes=60 * 1024 * 1024),
        name="write_out",
    )(*outs)
    return tuple(o[None, None] for o in outs)


def solution(mesh):
    u2, i2 = P("row", "col"), P("col", "row")
    return jax.shard_map(
        local,
        mesh=mesh,
        in_specs=(u2, i2, u2, i2, u2, u2, u2, u2, u2, u2, u2),
        out_specs=(u2, i2, u2, i2),
        check_vma=False,
    )
```

```python
import jax
import jax.numpy as jnp
from jax import lax
from jax.experimental import pallas as pl
from jax.experimental.pallas import tpu as pltpu
from jax.sharding import PartitionSpec as P

MESH = pl.DeviceIdType.MESH
F32, BF16, I32 = jnp.float32, jnp.bfloat16, jnp.int32
D = 128
TB = 128
UC = 32
HU = UC // 2
IC = 128
TILES = 48
BPR = 256
NX, NY, NZ = 8, 8, 8
TROWS = NX * NY * UC // TB
TCOLS = NZ * 2 * IC // TB

NEAR_FIRST = (0, 6, 1, 5, 2, 4, 3)
FAR_FIRST = (2, 1, 3, 0)
UNROLL = 16
ORDER_OUT = (3, 1, 2, 0)

SEM = pltpu.SemaphoreType.DMA


def each(n, body):
    lax.fori_loop(0, n, lambda i, c: (body(i), c)[1], 0)


def each_far_first(n, body):
    def one(i):
        off = lax.div(i + 1, 2)
        body(n // 2 + off * (1 - 2 * lax.rem(i, 2)))

    each(n, one)


def await_bytes(ref, sem):
    pltpu.make_async_copy(ref, ref, sem).wait()


def column(row, n, start=0):
    i = lax.broadcasted_iota(I32, (n, n), 0)
    j = lax.broadcasted_iota(I32, (n, n), 1)
    return jnp.sum(jnp.where(i == j, jnp.broadcast_to(row, (n, n)), 0), axis=1, keepdims=True)


def inv_sqrt(x):
    y = lax.rsqrt(x)
    return y * (1.5 - 0.5 * x * y * y)


def slot_order(key_row, other_row, live, order_ref):
    n = TILES
    key_row = jnp.where(live, key_row, 1024)
    key = column(key_row, n)
    other = column(other_row, n)
    sub = lax.broadcasted_iota(I32, (n, n), 0)
    lane = lax.broadcasted_iota(I32, (n, n), 1)
    rows = jnp.broadcast_to(key_row, (n, n))
    tied = (rows == key) & (lane < sub)
    rank = jnp.sum(jnp.where((rows < key) | tied, 1, 0), axis=1, keepdims=True)
    follows = jnp.max(jnp.where(tied, 1, 0), axis=1, keepdims=True)
    place = lax.broadcasted_iota(I32, (n, 128), 1)
    slot = lax.broadcasted_iota(I32, (n, 128), 0)
    hit = place == rank
    order_ref[0:1, :] = jnp.sum(jnp.where(hit, slot, 0), axis=0, keepdims=True)
    order_ref[1:2, :] = jnp.sum(jnp.where(hit, other, 0), axis=0, keepdims=True)
    order_ref[2:3, :] = jnp.sum(jnp.where(hit, follows, 0), axis=0, keepdims=True)
    upto = jnp.sum(jnp.where(key <= place, 1, 0), axis=0, keepdims=True)
    order_ref[3:4, :] = jnp.maximum(upto - 1, 0)
    order_ref[4:5, :] = jnp.max(jnp.where(key == place, 1, 0), axis=0, keepdims=True)


def kernel(
    users_h, items_h, udeg_h, ideg_h, tiles_h, trows_h, tcols_h, tcount_h, bu_h, bp_h, bn_h,
    user_out_h, item_out_h, grad_users_h, grad_items_h,
    user_out, item_out, grad_users, grad_items,
    users, items, udeg, ideg, tv, trows, tcols, tcount, bu, bp, bn,
    tt, ordr_v, ordc_v, ordr, ordc, part,
    huT, hu, hdT, hd, upad,
    uf0, uf1, itf0, itf1,
    pu0, pu1, pi0, pi1,
    ra0, rb0, ra1, rb1,
    sa0, sb0, sa1, sb1,
    qa0, qb0, qa1, qb1,
    rp0, rp1, si0, si1, si1f, rz0, rz1,
    load_sem, ag_sem, ag_xs, ag_ys, ag_zs, rs_sem, rs_as, rs_bs, rs_ps,
):
    r = lax.axis_index("row")
    c = lax.axis_index("col")
    core = lax.rem(r, 2)
    z = lax.div(r, 2)
    x = lax.rem(c, NX)
    y = lax.div(c, NX)

    def at_x(k):
        xx = lax.rem(x + k, NX)
        return xx, (r, y * NX + xx)

    def at_y(k):
        yy = lax.rem(y + k, NY)
        return yy, (r, yy * NX + x)

    def at_z(k):
        zz = lax.rem(z + k, NZ)
        return zz, (zz * 2 + core, c)

    partner = (z * 2 + 1 - core, c)

    def send(src, dst, ssem, rsem, device):
        pltpu.make_async_remote_copy(
            src_ref=src, dst_ref=dst, send_sem=ssem, recv_sem=rsem, device_id=device, device_id_type=MESH
        ).start()

    pairs = (
        (users_h, users), (items_h, items), (udeg_h, udeg), (ideg_h, ideg), (tiles_h, tv), (trows_h, trows),
        (tcols_h, tcols), (tcount_h, tcount), (bu_h, bu), (bp_h, bp), (bn_h, bn),
    )
    loads = [pltpu.make_async_copy(src, dst, load_sem.at[n]) for n, (src, dst) in enumerate(pairs)]
    for n in (2, 3, 0, 1, 5, 6, 7, 4, 8, 9, 10):
        loads[n].start()

    barrier = pltpu.get_barrier_semaphore()

    def greet(device):
        pl.semaphore_signal(barrier, inc=1, device_id=device, device_id_type=MESH)

    each_far_first(NX - 1, lambda k: [greet(at_x(k + 1)[1]), greet(at_y(k + 1)[1]), greet(at_z(k + 1)[1])])
    greet(partner)

    for n in range(4):
        loads[n].wait()
    du = inv_sqrt(column(udeg[...], UC).astype(F32))
    di = inv_sqrt(column(ideg[...], IC).astype(F32))

    def gather_start(q, uf, itf, user_val, item_val):
        s = ag_sem.at[q]
        mine_u = uf.at[y, x]
        mine_i = itf.at[z, core]
        itf[z, core] = (item_val() * di).astype(BF16)
        if q == 0:
            uf[y, x] = (user_val() * du).astype(BF16)
            pl.semaphore_wait(barrier, NX + NY + NZ - 2)
        each_far_first(NZ - 1, lambda k: send(mine_i, mine_i, s.at[0], ag_zs.at[q, k], at_z(k + 1)[1]))
        if q == 1:
            uf[y, x] = (user_val() * du).astype(BF16)

        def one(k):
            send(mine_u, mine_u, s.at[3], ag_xs.at[q, k], at_x(k + 1)[1])
            send(mine_u, mine_u, s.at[5], ag_ys.at[q, k], at_y(k + 1)[1])

        each_far_first(NX - 1, one)
        send(mine_i, mine_i, s.at[1], s.at[2], partner)

    def gather_second(q, uf):
        s = ag_sem.at[q]
        for k in NEAR_FIRST:
            xx = lax.rem(x + NX - 1 - k, NX)
            await_bytes(uf.at[y, xx], ag_xs.at[q, k])
            half = uf.at[y, xx, 0:HU]
            each_far_first(NY - 1, lambda j: send(half, half, s.at[7], s.at[8], at_y(j + 1)[1]))
            yy = lax.rem(y + NY - 1 - k, NY)
            await_bytes(uf.at[yy, x], ag_ys.at[q, k])
            other = uf.at[yy, x, HU:UC]
            each_far_first(NX - 1, lambda j: send(other, other, s.at[9], s.at[10], at_x(j + 1)[1]))

    def gather_forward(q, itf):
        s = ag_sem.at[q]
        for k in NEAR_FIRST:
            zz = lax.rem(z + NZ - 1 - k, NZ)
            got = itf.at[zz, core]
            await_bytes(got, ag_zs.at[q, k])
            send(got, got, s.at[1], s.at[2], partner)

    def gather_items_done(q, itf):
        await_bytes(itf.at[:, 0], ag_sem.at[q, 2])

    def gather_users_done(q, uf):
        await_bytes(uf.at[0 : NY - 1, 0 : NX - 1, 0:HU], ag_sem.at[q, 8])
        await_bytes(uf.at[0 : NY - 1, 0 : NX - 1, HU:UC], ag_sem.at[q, 10])

    def gather_sent(q, uf, itf):
        s = ag_sem.at[q]
        await_bytes(itf.at[0 : NZ - 1, 0], s.at[0])
        await_bytes(itf.at[:, 0], s.at[1])
        await_bytes(uf.at[0, 0 : NX - 1], s.at[3])
        await_bytes(uf.at[0 : NY - 1, 0], s.at[5])
        await_bytes(uf.at[0 : NY - 1, 0 : NX - 1, 0:HU], s.at[7])
        await_bytes(uf.at[0 : NY - 1, 0 : NX - 1, HU:UC], s.at[9])

    def user_side(itf, pu):
        def one(j, acc):
            other = ordr[1, j]
            block = itf[lax.div(other, 2), lax.rem(other, 2)]
            prod = jnp.dot(tv[ordr[0, j]], block, preferred_element_type=F32)
            acc = acc * ordr[2, j].astype(F32) + prod
            part[j] = acc
            return acc

        lax.fori_loop(0, TILES, one, jnp.zeros((TB, D), F32), unroll=UNROLL)

        def place(t):
            whole = part[ordr[3, t]] * ordr[4, t].astype(F32)
            per = NX * UC // TB
            cols = TB // UC
            yy = lax.div(t, per)
            xx = lax.rem(t, per) * cols
            pu[yy, pl.ds(xx, cols)] = whole.reshape(cols, UC, D).astype(pu.dtype)

        each(TROWS, place)

    def item_side(uf, pi):
        def one(j, acc):
            t = ordc[1, j]
            per = NX * UC // TB
            cols = TB // UC
            block = uf[lax.div(t, per), pl.ds(lax.rem(t, per) * cols, cols)].reshape(TB, D)
            prod = jnp.dot(tt[j], block, preferred_element_type=F32)
            acc = acc * ordc[2, j].astype(F32) + prod
            part[j] = acc
            return acc

        lax.fori_loop(0, TILES, one, jnp.zeros((TB, D), F32), unroll=UNROLL)

        def place(t):
            pi[lax.div(t, 2), lax.rem(t, 2)] = part[ordc[3, t]] * ordc[4, t].astype(F32)

        each(TCOLS, place)

    def scatter_users_first(q, pu, ra, rb):
        s = rs_sem.at[q]
        for step in FAR_FIRST:
            px = lax.rem(lax.div(x, 2) + step, NX // 2)
            py = lax.rem(lax.div(y, 2) + step, NY // 2)

            def one(k):
                yy, dev = at_y(k + 1)
                send(pu.at[yy, pl.ds(px * 2, 2), 0:HU], ra.at[px, k], s.at[0], rs_as.at[q, px], dev)
                xx, dev = at_x(k + 1)
                send(pu.at[pl.ds(py * 2, 2), xx, HU:UC], rb.at[py, k], s.at[2], rs_bs.at[q, py], dev)

            each_far_first(NY - 1, one)

    def scatter_users_second(q, pu, ra, rb, sa, sb, qa, qb):
        s = rs_sem.at[q]
        for step in FAR_FIRST:
            px = lax.rem(lax.div(x, 2) + step, NX // 2)
            py = lax.rem(lax.div(y, 2) + step, NY // 2)

            def to_x(xx):
                k = lax.rem(xx - x + NX, NX) - 1
                send(sa.at[xx], qa.at[k], s.at[4], s.at[5], (r, y * NX + xx))

            def to_y(yy):
                k = lax.rem(yy - y + NY, NY) - 1
                send(sb.at[yy], qb.at[k], s.at[6], s.at[7], (r, yy * NX + x))

            await_bytes(ra.at[px], rs_as.at[q, px])
            two = pl.ds(px * 2, 2)
            sa[two] = pu[y, two, 0:HU].astype(F32) + jnp.sum(ra[px].astype(F32), axis=0)
            if step:
                to_x(px * 2)
                to_x(px * 2 + 1)
            else:
                to_x(px * 4 + 1 - x)
            await_bytes(rb.at[py], rs_bs.at[q, py])
            two = pl.ds(py * 2, 2)
            sb[two] = pu[two, x, HU:UC].astype(F32) + jnp.sum(rb[py].astype(F32), axis=0)
            if step:
                to_y(py * 2)
                to_y(py * 2 + 1)
            else:
                to_y(py * 4 + 1 - y)

    def scatter_users_done(q, sa, sb, qa, qb):
        s = rs_sem.at[q]
        await_bytes(qa, s.at[5])
        await_bytes(qb, s.at[7])
        first = sa[x] + jnp.sum(qa[...], axis=0)
        second = sb[y] + jnp.sum(qb[...], axis=0)
        return jnp.concatenate([first, second], axis=0) * du

    def scatter_users_sent(q, ra, rb, qa, qb):
        s = rs_sem.at[q]
        await_bytes(ra, s.at[0])
        await_bytes(rb, s.at[2])
        await_bytes(qa, s.at[4])
        await_bytes(qb, s.at[6])

    def scatter_items_first(q, pi, rp):
        s = rs_sem.at[q]

        def one(k):
            zz = lax.rem(z + 1 + k, NZ)
            send(pi.at[zz, 1 - core], rp.at[zz], s.at[8], rs_ps.at[q, k], partner)

        each_far_first(NZ - 1, one)
        one(NZ - 1)

    def scatter_items_second(q, pi, rp, si, keep, rz):
        s = rs_sem.at[q]

        def one(k):
            zz, dev = at_z(k + 1)
            await_bytes(rp.at[zz], rs_ps.at[q, k])
            si[zz] = (pi[zz, core] + rp[zz]).astype(si.dtype)
            send(si.at[zz], rz.at[k], s.at[9], s.at[10], dev)

        each_far_first(NZ - 1, one)
        await_bytes(rp.at[z], rs_ps.at[q, NZ - 1])
        keep[...] = pi[z, core] + rp[z]

    def scatter_items_done(q, keep, rz):
        await_bytes(rz, rs_sem.at[q, 10])
        return (keep[...] + jnp.sum(rz[...].astype(F32), axis=0)) * di

    def scatter_items_sent(q, rp, rz):
        await_bytes(rp, rs_sem.at[q, 8])
        await_bytes(rz, rs_sem.at[q, 9])

    def products(q, uf, itf, pu, pi, ra, rb, rp, si, keep, rz):
        gather_items_done(q, itf)
        user_side(itf, pu)
        scatter_users_first(q, pu, ra, rb)
        gather_users_done(q, uf)
        item_side(uf, pi)
        scatter_items_first(q, pi, rp)
        scatter_items_second(q, pi, rp, si, keep, rz)

    gather_start(0, uf0, itf0, lambda: users[...].astype(F32), lambda: items[...].astype(F32))
    for n in range(5, 8):
        loads[n].wait()
    live = lax.broadcasted_iota(I32, (1, TILES), 1) < jnp.broadcast_to(tcount[...], (1, TILES))
    slot_order(trows[...], tcols[...], live, ordr_v)
    slot_order(tcols[...], trows[...], live, ordc_v)
    copy_r = pltpu.make_async_copy(ordr_v, ordr, load_sem.at[11])
    copy_c = pltpu.make_async_copy(ordc_v, ordc, load_sem.at[12])
    copy_r.start()
    copy_c.start()
    gather_second(0, uf0)
    copy_r.wait()
    copy_c.wait()
    loads[4].wait()

    def turn(j):
        tt[j] = tv[ordc[0, j]].T

    each(TILES, turn)
    for n in range(8, 11):
        loads[n].wait()
    ids = lax.broadcasted_iota(I32, (IC, BPR), 0)
    hot_u = jnp.where(ids == bu[...], 1.0, 0.0)
    hot_d = jnp.where(ids == bp[...], 1.0, 0.0) - jnp.where(ids == bn[...], 1.0, 0.0)
    huT[...] = hot_u[0:UC].astype(BF16)
    hdT[...] = hot_d.astype(BF16)
    hu[...] = hot_u.T.astype(BF16)
    hd[...] = hot_d.T.astype(BF16)
    gather_forward(0, itf0)
    products(0, uf0, itf0, pu0, pi0, ra0, rb0, rp0, si0, si0.at[z], rz0)
    scatter_users_second(0, pu0, ra0, rb0, sa0, sb0, qa0, qb0)
    u_out = scatter_users_done(0, sa0, sb0, qa0, qb0).astype(BF16)
    i_out = scatter_items_done(0, si0.at[z], rz0).astype(BF16)
    user_out[...] = u_out
    item_out[...] = i_out
    stores = [
        pltpu.make_async_copy(src, dst, load_sem.at[13 + n])
        for n, (src, dst) in enumerate(
            ((user_out, user_out_h), (item_out, item_out_h), (grad_users, grad_users_h), (grad_items, grad_items_h))
        )
    ]
    stores[0].start()
    stores[1].start()

    upad[0:UC] = u_out
    upad[UC:IC] = jnp.zeros((IC - UC, D), BF16)
    u_vec = jnp.dot(hu[...], upad[...], preferred_element_type=F32)
    d_vec = jnp.dot(hd[...], i_out, preferred_element_type=F32)
    score = jnp.sum(u_vec * d_vec, axis=1, keepdims=True)
    weight = -jax.nn.sigmoid(-score)

    def spread(hotT, v):
        hi = v.astype(BF16)
        lo = (v - hi.astype(F32)).astype(BF16)
        return jnp.dot(hotT, hi, preferred_element_type=F32) + jnp.dot(hotT, lo, preferred_element_type=F32)

    gather_start(
        1, uf1, itf1, lambda: spread(huT[...], weight * d_vec), lambda: spread(hdT[...], weight * u_vec)
    )
    gather_second(1, uf1)
    gather_forward(1, itf1)
    products(1, uf1, itf1, pu1, pi1, ra1, rb1, rp1, si1, si1f, rz1)
    scatter_users_second(1, pu1, ra1, rb1, sa1, sb1, qa1, qb1)
    grad_items[...] = scatter_items_done(1, si1f, rz1)
    stores[3].start()
    grad_users[...] = scatter_users_done(1, sa1, sb1, qa1, qb1)
    stores[2].start()

    gather_sent(0, uf0, itf0)
    gather_sent(1, uf1, itf1)
    scatter_users_sent(0, ra0, rb0, qa0, qb0)
    scatter_users_sent(1, ra1, rb1, qa1, qb1)
    scatter_items_sent(0, rp0, rz0)
    scatter_items_sent(1, rp1, rz1)
    for one in stores:
        one.wait()


def write_out(a, b, c, d, ah, bh, ch, dh, av, bv, cv, dv, sem):
    triples = ((a, av, ah), (b, bv, bh), (c, cv, ch), (d, dv, dh))
    reads = [pltpu.make_async_copy(src, mid, sem.at[n]) for n, (src, mid, _) in enumerate(triples)]
    writes = [pltpu.make_async_copy(mid, dst, sem.at[n + 4]) for n, (_, mid, dst) in enumerate(triples)]
    for n in ORDER_OUT:
        reads[n].start()
    for n in ORDER_OUT:
        reads[n].wait()
        writes[n].start()
    for n in ORDER_OUT:
        writes[n].wait()


def local(users, items, udeg, ideg, tiles, trows, tcols, tcount, bu, bp, bn):
    hbm = pl.BlockSpec(memory_space=pltpu.HBM)
    V = pltpu.VMEM
    order = (8, 128)
    fields = (NY, NX, UC, D)
    fieldi = (NZ, 2, IC, D)
    out_shape = (
        jax.ShapeDtypeStruct((UC, D), BF16),
        jax.ShapeDtypeStruct((IC, D), BF16),
        jax.ShapeDtypeStruct((UC, D), F32),
        jax.ShapeDtypeStruct((IC, D), F32),
    )
    args = (users[0, 0], items[0, 0], udeg[0], ideg[0], tiles[0, 0], trows[0], tcols[0], tcount, bu[0], bp[0], bn[0])
    outs = pl.pallas_call(
        kernel,
        out_shape=out_shape,
        in_specs=[hbm] * 11,
        out_specs=(hbm,) * 4,
        scratch_shapes=[V(o.shape, o.dtype) for o in out_shape]
        + [V(a.shape, a.dtype) for a in args]
        + [
            V((TILES, TB, TB), BF16),
            V(order, I32),
            V(order, I32),
            pltpu.SMEM(order, I32),
            pltpu.SMEM(order, I32),
            V((TILES, TB, D), F32),
            V((UC, BPR), BF16),
            V((BPR, IC), BF16),
            V((IC, BPR), BF16),
            V((BPR, IC), BF16),
            V((IC, D), BF16),
            V(fields, BF16),
            V(fields, BF16),
            V(fieldi, BF16),
            V(fieldi, BF16),
            V(fields, F32),
            V(fields, BF16),
            V(fieldi, F32),
            V(fieldi, F32),
            V((NX // 2, NY - 1, 2, HU, D), F32),
            V((NY // 2, NX - 1, 2, HU, D), F32),
            V((NX // 2, NY - 1, 2, HU, D), BF16),
            V((NY // 2, NX - 1, 2, HU, D), BF16),
            V((NX, HU, D), F32),
            V((NY, HU, D), F32),
            V((NX, HU, D), F32),
            V((NY, HU, D), F32),
            V((NX - 1, HU, D), F32),
            V((NY - 1, HU, D), F32),
            V((NX - 1, HU, D), F32),
            V((NY - 1, HU, D), F32),
            V((NZ, IC, D), F32),
            V((NZ, IC, D), F32),
            V((NZ, IC, D), F32),
            V((NZ, IC, D), BF16),
            V((IC, D), F32),
            V((NZ - 1, IC, D), F32),
            V((NZ - 1, IC, D), BF16),
            SEM((17,)),
            SEM((2, 11)),
            SEM((2, NX - 1)),
            SEM((2, NY - 1)),
            SEM((2, NZ - 1)),
            SEM((2, 11)),
            SEM((2, NX // 2)),
            SEM((2, NY // 2)),
            SEM((2, NZ)),
        ],
        compiler_params=pltpu.CompilerParams(
            collective_id=0, has_side_effects=True, vmem_limit_bytes=60 * 1024 * 1024
        ),
        name="lightgcn",
    )(*args)
    outs = pl.pallas_call(
        write_out,
        out_shape=out_shape,
        in_specs=[hbm] * 4,
        out_specs=(hbm,) * 4,
        scratch_shapes=[V(o.shape, o.dtype) for o in out_shape] + [SEM((8,))],
        compiler_params=pltpu.CompilerParams(vmem_limit_bytes=60 * 1024 * 1024),
        name="write_out",
    )(*outs)
    return tuple(o[None, None] for o in outs)


def solution(mesh):
    u2, i2 = P("row", "col"), P("col", "row")
    return jax.shard_map(
        local,
        mesh=mesh,
        in_specs=(u2, i2, u2, i2, u2, u2, u2, u2, u2, u2, u2),
        out_specs=(u2, i2, u2, i2),
        check_vma=False,
    )
```
